32 devices in a mesh: mem: 4 (over y, x), reg: 8 (over z, core).
Axes of the slice: x: 2, y: 2, z: 4, core: 2. Of those that a mesh axis runs over, the one named last changes fastest.
Arguments:
- prior_states: bfloat16 [256, 227, 1024], P('mem', None, 'reg'), may hold values from -6 to 6
- sensor_space_runs: bfloat16 [256, 8, 8192], P('mem', 'reg'), may hold values from -6 to 6
- sensor_readings: float32 [8, 8192], P('reg'), may hold values from -8 to 8
- noise_precision: float32 [8, 8192], P('reg'), may hold values from 0.1 to 1
- reading_pointers: int32 [8, 4, 4, 512], P('reg', 'mem'), may hold values from 0 to 8703, as said below
- reading_tally: int32 [8, 4, 4], P('reg', 'mem'), may hold values from 128 to 512, as said below
Outputs:
- analysis: bfloat16 [256, 227, 1024], P('mem', None, 'reg')
The draws below stay inside these ranges and needn't reach their ends.
Inputs may be any that keep to these rules, and one draw needn't show every extreme that they name: Row reading_pointers[r, m, g, :] holds 512 distinct positions of region r's extended observations, together one window of 512 consecutive positions, in an order drawn from the seed. A local analysis uses the first reading_tally[r, m, g] entries of its list.
All inputs are finite; a program needn't handle non-finite values.
Results may differ from the reference program's by a relative error of at most 0.009.
Values may be sent and summed in bfloat16 or wider, within the bound.
A program may use at most 128 MiB of HBM per device.

```python
import math
import jax
import jax.numpy as jnp
from jax import lax

RUN_AMOUNT = 256
FIELDS_PER_SITE = 227
PILLARS_PER_PATCH = 8
LMAX = 512
NOBS_R = 8192
NS_ITERS = 6
GROUPS = 4
BLOCKS = 4
REGIONS = 8
HW = 256
GRID_PILLARS = 1024


def draw_reading_pointers(key, part):
    block_total = BLOCKS * GROUPS
    positions = jnp.arange(block_total, dtype=jnp.int32)
    starts = positions * (NOBS_R + 2 * HW - LMAX) // (block_total - 1)
    keys = jax.random.split(key, REGIONS * block_total)
    orders = jax.vmap(lambda single: jax.random.permutation(single, LMAX))(keys)
    orders = orders.reshape(REGIONS, block_total, LMAX).astype(jnp.int32)
    listed = starts[None, :, None] + orders
    return listed.reshape(REGIONS, BLOCKS, GROUPS, LMAX).astype(jnp.int32)


def draw_reading_tally(key, part):
    entries = REGIONS * BLOCKS * GROUPS
    first_key, second_key = jax.random.split(key)
    counted = jax.random.randint(first_key, (entries,), LMAX // 4, LMAX + 1, dtype=jnp.int32)
    chosen = jax.random.randint(second_key, (), 0, entries, dtype=jnp.int32)
    positions = jnp.arange(entries, dtype=jnp.int32)
    counted = jnp.where(positions == chosen, LMAX, counted)
    counted = jnp.where(positions == (chosen + 1) % entries, LMAX // 4, counted)
    return counted.reshape(REGIONS, BLOCKS, GROUPS).astype(jnp.int32)


def shard_levels(rng, dims, pieces, least, top_value):
    loudness = 1.0
    for dim, parts in pieces:
        heights = jax.random.uniform(jax.random.fold_in(jax.random.fold_in(rng, 6), dim), (parts,), jnp.float32, least / len(pieces), top_value / len(pieces))
        loudness = loudness * jnp.repeat(jnp.exp(heights), dims[dim] // parts).reshape((-1,) + (1,) * (len(dims) - 1 - dim))
    return loudness


def bell_draw(stream_key, dims, spread, bound, pieces=(), kind=jnp.bfloat16):
    drawn = spread * jax.random.normal(stream_key, dims, jnp.float32)
    if pieces:
        drawn = drawn * shard_levels(stream_key, dims, pieces, -0.22, 0.18)
    return jnp.clip(drawn, -bound, bound).astype(kind)


def setup_inputs(seed: int = 0) -> dict:
    key_of = jax.random.split(jax.random.key(seed), 7)
    return {
        "prior_states": bell_draw(key_of[0], (RUN_AMOUNT, FIELDS_PER_SITE, GRID_PILLARS), 1.0, 6.0, ((0, 4), (2, 8))),
        "sensor_space_runs": bell_draw(key_of[1], (RUN_AMOUNT, REGIONS, NOBS_R), 1.0, 6.0, ((0, 4), (1, 8))),
        "sensor_readings": bell_draw(key_of[2], (REGIONS, NOBS_R), 1.5, 8.0, ((0, 8),), jnp.float32),
        "noise_precision": jnp.clip(jnp.exp(math.log(1.0) - 2.3025851 * jax.random.uniform(key_of[3], (REGIONS, NOBS_R), jnp.float32) ** shard_levels(key_of[3], (REGIONS, NOBS_R), ((0, 8),), -0.2, 0.2)), 0.1, 1.0),
        "reading_pointers": draw_reading_pointers(jax.random.fold_in(key_of[6], 71), 0),
        "reading_tally": draw_reading_tally(jax.random.fold_in(key_of[6], 71), 0),
    }


inflation = 1.1
highest = lax.Precision.HIGHEST

def nearby_correction(prior_patch, sensor_space_lines, sensor_readings, precision_nearby, pending_amount):
    runs_sequence = prior_patch.shape[0]
    prior_states_narrow = prior_patch.astype(jnp.float32)
    middle_pillar = lax.optimization_barrier(jnp.mean(prior_states_narrow, axis=0))
    deviation_matrix = (prior_states_narrow - middle_pillar[None]).astype(jnp.bfloat16)
    observed_f32 = sensor_space_lines.astype(jnp.float32)
    ens_mean = lax.optimization_barrier(jnp.mean(observed_f32, axis=0))
    anomaly = lax.optimization_barrier((observed_f32 - ens_mean[None]).astype(jnp.bfloat16)).astype(jnp.float32)
    active = (jnp.arange(sensor_space_lines.shape[1], dtype=jnp.int32) < pending_amount).astype(jnp.float32)
    weight = precision_nearby * active
    identity = jnp.eye(runs_sequence, dtype=jnp.float32)
    gram_matrix = jnp.dot(anomaly, (anomaly * weight[None, :]).T, precision=highest) + (runs_sequence - 1) / inflation * identity
    innovation_sum = jnp.dot(anomaly, weight * (sensor_readings - ens_mean), precision=highest)
    frobenius = jnp.sqrt(jnp.sum(gram_matrix * gram_matrix))
    iterate = gram_matrix / frobenius
    inverse_root = identity
    for iteration in range(NS_ITERS):
        factor = 1.5 * identity - 0.5 * jnp.dot(inverse_root, iterate, precision=highest)
        iterate = jnp.dot(iterate, factor, precision=highest)
        inverse_root = jnp.dot(factor, inverse_root, precision=highest)
    inverse_root = inverse_root / jnp.sqrt(frobenius)
    mean_weight = jnp.dot(inverse_root, jnp.dot(inverse_root, innovation_sum, precision=highest), precision=highest)
    transform = (math.sqrt(runs_sequence - 1) * inverse_root + mean_weight[:, None]).astype(jnp.bfloat16)
    combined = jnp.einsum('jvc,jk->kvc', deviation_matrix.astype(jnp.float32), transform.astype(jnp.float32), precision=highest)
    return (middle_pillar[None] + combined).astype(jnp.bfloat16)

def extend_regions(values):
    before = jnp.roll(values, 1, axis=-2)[..., -HW:]
    after = jnp.roll(values, -1, axis=-2)[..., :HW]
    return jnp.concatenate([before, values, after], axis=-1)

def reference(prior_states, sensor_space_runs, sensor_readings, noise_precision, reading_pointers, reading_tally):
    extended = extend_regions(sensor_space_runs)
    statistics = extend_regions(jnp.stack([sensor_readings, noise_precision]))
    flat_lists = reading_pointers.reshape(-1, LMAX)
    flat_counts = reading_tally.reshape(-1)
    group_total = flat_counts.shape[0]
    per_region = BLOCKS * GROUPS

    def analyse_group(patch_offset):
        region = patch_offset // per_region
        indices = lax.dynamic_index_in_dim(flat_lists, patch_offset, 0, keepdims=False)
        region_ens = lax.dynamic_index_in_dim(extended, region, 1, keepdims=False)
        sensor_space_lines = jnp.take(region_ens, indices, axis=1)
        region_stats = lax.dynamic_index_in_dim(statistics, region, 1, keepdims=False)
        chosen_moments = jnp.take(region_stats, indices, axis=1)
        prior_patch = lax.dynamic_slice_in_dim(prior_states, patch_offset * PILLARS_PER_PATCH, PILLARS_PER_PATCH, axis=2)
        pending_amount = lax.dynamic_index_in_dim(flat_counts, patch_offset, 0, keepdims=False)
        return nearby_correction(prior_patch, sensor_space_lines, chosen_moments[0], chosen_moments[1], pending_amount)
    analysed = lax.map(analyse_group, jnp.arange(group_total, dtype=jnp.int32))
    return jnp.transpose(analysed, (1, 2, 0, 3)).reshape(RUN_AMOUNT, FIELDS_PER_SITE, group_total * PILLARS_PER_PATCH)
```

```python
import functools
import math

import jax
import jax.numpy as jnp
from jax import lax
from jax.experimental import pallas as pl
from jax.experimental.pallas import tpu as pltpu
from jax.sharding import PartitionSpec as P

NS_ITERS = 6
HW = 256
LANES = 128
CHUNKS = 4
VMEM_LIMIT = 60 * 1024 * 1024

inflation = 1.1
highest = lax.Precision.HIGHEST
MESH = pl.DeviceIdType.MESH


def lane_part(shape, width):
    return lax.broadcasted_iota(jnp.int32, shape, len(shape) - 1) // width


def swap_lane_parts(pieces, width):
    parts = len(pieces)
    part = lane_part(pieces[0].shape, width)
    swapped = []
    for d in range(parts):
        result = pieces[d]
        for s in range(parts):
            if s != d:
                moved = pltpu.roll(pieces[s], (s - d) * width % LANES, 1)
                result = jnp.where(part == s, moved, result)
        swapped.append(result)
    return swapped


def pack_kernel(states_ref, packed_ref):
    fields, _, columns = states_ref.shape
    blocks, rows, _, _ = packed_ref.shape
    width = columns // blocks
    parts = LANES // width

    def body(r, carry):
        for tile in range(columns // LANES):
            lanes = slice(tile * LANES, (tile + 1) * LANES)
            pieces = [
                states_ref[jnp.minimum(s * rows + r, fields - 1), :, lanes].astype(jnp.float32)
                for s in range(parts)
            ]
            for d, piece in enumerate(swap_lane_parts(pieces, width)):
                packed_ref[tile * parts + d, r] = piece.astype(jnp.bfloat16)
        return carry

    lax.fori_loop(0, rows, body, 0)


def pack(states, blocks):
    fields, runs, columns = states.shape
    rows = -(-fields // (LANES // (columns // blocks)))
    return pl.pallas_call(
        pack_kernel,
        out_shape=jax.ShapeDtypeStruct((blocks, rows, runs, LANES), jnp.bfloat16),
        in_specs=[pl.BlockSpec(memory_space=pltpu.VMEM)],
        out_specs=pl.BlockSpec(memory_space=pltpu.VMEM),
        compiler_params=pltpu.CompilerParams(vmem_limit_bytes=VMEM_LIMIT),
        name="pack_columns",
    )(states)


def window_kernel(starts_ref, before_ref, own_ref, after_ref, windows_ref, extended):
    width = before_ref.shape[1]
    own = own_ref.shape[1]
    length = windows_ref.shape[2]
    extended[:, :width] = before_ref[...]
    extended[:, width : width + own] = own_ref[...]
    extended[:, width + own :] = after_ref[...]
    span = length + LANES
    last = extended.shape[1] - span

    def body(w, carry):
        start = starts_ref[w]
        base = pl.multiple_of(jnp.minimum(start // LANES * LANES, last), LANES)
        wide = extended[:, pl.ds(base, span)].astype(jnp.float32)
        turned = pltpu.roll(wide, lax.rem(span - (start - base), span), 1)
        windows_ref[w] = turned[:, :length].astype(jnp.bfloat16)
        return carry

    lax.fori_loop(0, windows_ref.shape[0], body, 0)


def cut_windows(starts, before, own, after, length):
    runs, own_width = own.shape
    return pl.pallas_call(
        window_kernel,
        out_shape=jax.ShapeDtypeStruct((starts.shape[0], runs, length), jnp.bfloat16),
        in_specs=[pl.BlockSpec(memory_space=pltpu.SMEM)]
        + [pl.BlockSpec(memory_space=pltpu.VMEM)] * 3,
        out_specs=pl.BlockSpec(memory_space=pltpu.VMEM),
        scratch_shapes=[pltpu.VMEM((runs, own_width + 2 * before.shape[1]), jnp.bfloat16)],
        compiler_params=pltpu.CompilerParams(vmem_limit_bytes=VMEM_LIMIT),
        name="cut_windows",
    )(starts, before, own, after)


def chunk_bounds(rows):
    edges = [rows * i // CHUNKS for i in range(CHUNKS + 1)]
    return list(zip(edges[:-1], edges[1:]))


def apply_rows(transform_ref, states_ref, result_ref, first, last, patch, groups):
    blocks, _, runs, _ = states_ref.shape
    members = blocks * runs

    def one(r):
        x = jnp.concatenate([states_ref[b, r] for b in range(blocks)], axis=0)
        x = x.astype(jnp.float32)
        center = jnp.sum(x, axis=0, keepdims=True) * (1.0 / members)
        pert = (x - center).astype(jnp.bfloat16).astype(jnp.float32)
        group = lane_part(pert.shape, patch) % groups
        masked = [jnp.where(group == g, pert, 0.0).astype(jnp.bfloat16) for g in range(groups)]
        return center, jnp.concatenate(masked, axis=0)

    def body(i, carry):
        r0 = first + 2 * i
        r1 = jnp.minimum(r0 + 1, last - 1)
        center0, masked0 = one(r0)
        center1, masked1 = one(r1)
        moved = jnp.dot(
            transform_ref[...],
            jnp.concatenate([masked0, masked1], axis=1),
            preferred_element_type=jnp.float32,
        )
        for r, center, lanes in ((r0, center0, slice(0, LANES)), (r1, center1, slice(LANES, None))):
            analysed = (moved[:, lanes] + center).astype(jnp.bfloat16)
            for b in range(blocks):
                result_ref[b, r] = analysed[b * runs : (b + 1) * runs]
        return carry

    lax.fori_loop(0, (last - first + 1) // 2, body, 0)


def unpack_row(received, result_ref, r, valid):
    blocks, rows, _, _ = received.shape
    columns = result_ref.shape[2]
    width = columns // blocks
    parts = LANES // width
    for tile in range(columns // LANES):
        lanes = slice(tile * LANES, (tile + 1) * LANES)
        pieces = [received[tile * parts + d, r].astype(jnp.float32) for d in range(parts)]
        swapped = swap_lane_parts(pieces, width)
        for s in range(valid):
            result_ref[s * rows + r, :, lanes] = swapped[s].astype(jnp.bfloat16)


def unpack_rows(received, result_ref, first, last):
    rows = received.shape[1]
    fields = result_ref.shape[0]
    parts = LANES // (result_ref.shape[2] // received.shape[0])
    whole = rows - (parts * rows - fields)

    def body(r, carry):
        unpack_row(received, result_ref, r, parts)
        return carry

    lax.fori_loop(first, min(last, whole), body, 0)
    for r in range(max(first, whole), last):
        unpack_row(received, result_ref, r, parts - 1)


def analysis_kernel(
    patch, groups, transform_ref, states_ref, result_ref, outgoing, received, send_sem, recv_sem
):
    blocks, rows, _, _ = states_ref.shape
    me = lax.axis_index("mem")
    barrier = pltpu.get_barrier_semaphore()
    for k in range(1, blocks):
        pl.semaphore_signal(
            barrier, inc=1, device_id={"mem": lax.rem(me + k, blocks)}, device_id_type=MESH
        )
    pl.semaphore_wait(barrier, blocks - 1)

    copies = []
    for c, (first, last) in enumerate(chunk_bounds(rows)):
        apply_rows(transform_ref, states_ref, outgoing, first, last, patch, groups)
        started = []
        for k in range(1, blocks):
            peer = lax.rem(me + k, blocks)
            copy = pltpu.make_async_remote_copy(
                src_ref=outgoing.at[peer, pl.ds(first, last - first)],
                dst_ref=received.at[me, pl.ds(first, last - first)],
                send_sem=send_sem.at[k - 1, c],
                recv_sem=recv_sem.at[k - 1, c],
                device_id={"mem": peer},
                device_id_type=MESH,
            )
            copy.start()
            started.append(copy)
        received[me, pl.ds(first, last - first)] = outgoing[me, pl.ds(first, last - first)]
        copies.append(started)
    for (first, last), started in zip(chunk_bounds(rows), copies):
        for copy in started:
            copy.wait_recv()
        unpack_rows(received, result_ref, first, last)
    for started in copies:
        for copy in started:
            copy.wait_send()


def analyse(transform, states, fields, columns, patch, groups):
    blocks, rows, runs, _ = states.shape
    return pl.pallas_call(
        functools.partial(analysis_kernel, patch, groups),
        out_shape=jax.ShapeDtypeStruct((fields, runs, columns), jnp.bfloat16),
        in_specs=[pl.BlockSpec(memory_space=pltpu.VMEM)] * 2,
        out_specs=pl.BlockSpec(memory_space=pltpu.VMEM),
        scratch_shapes=[
            pltpu.VMEM(states.shape, jnp.bfloat16),
            pltpu.VMEM(states.shape, jnp.bfloat16),
            pltpu.SemaphoreType.DMA((blocks - 1, CHUNKS)),
            pltpu.SemaphoreType.DMA((blocks - 1, CHUNKS)),
        ],
        compiler_params=pltpu.CompilerParams(
            collective_id=0, has_side_effects=True, vmem_limit_bytes=VMEM_LIMIT
        ),
        name="analyse_and_return",
    )(transform, states)


def from_neighbours(cells, width):
    count = lax.axis_size("reg")
    head, tail = cells[:, :width], cells[:, cells.shape[1] - width :]
    before = lax.ppermute(tail, "reg", [(i, (i + 1) % count) for i in range(count)])
    after = lax.ppermute(head, "reg", [((i + 1) % count, i) for i in range(count)])
    return before, after


def local_transform(lines, readings, weight):
    members = lines.shape[0]
    observed = lines.astype(jnp.float32)
    ens_mean = jnp.mean(observed, axis=0)
    anomaly = lax.optimization_barrier((observed - ens_mean[None]).astype(jnp.bfloat16)).astype(
        jnp.float32
    )
    identity = jnp.eye(members, dtype=jnp.float32)
    gram = (
        jnp.dot(anomaly, (anomaly * weight[None, :]).T, precision=highest)
        + (members - 1) / inflation * identity
    )
    innovation_sum = jnp.dot(anomaly, weight * (readings - ens_mean), precision=highest)
    frobenius = jnp.sqrt(jnp.sum(gram * gram))
    iterate = gram / frobenius
    dot = functools.partial(jnp.dot, precision=lax.Precision.HIGH)
    factor = 1.5 * identity - 0.5 * iterate
    inverse_root = factor
    for iteration in range(1, NS_ITERS):
        iterate = dot(iterate, factor)
        factor = 1.5 * identity - 0.5 * dot(inverse_root, iterate)
        inverse_root = dot(factor, inverse_root)
    inverse_root = inverse_root / jnp.sqrt(frobenius)
    mean_weight = jnp.dot(
        inverse_root, jnp.dot(inverse_root, innovation_sum, precision=highest), precision=highest
    )
    transform = math.sqrt(members - 1) * inverse_root + mean_weight[:, None]
    return transform.astype(jnp.bfloat16).T


def per_device(
    prior_states,
    sensor_space_runs,
    sensor_readings,
    noise_precision,
    reading_pointers,
    reading_tally,
):
    blocks = lax.axis_size("mem")
    runs, fields, columns = prior_states.shape
    members = runs * blocks
    groups = reading_tally.shape[2]
    patch = columns // blocks // groups
    packed = pack(jnp.transpose(prior_states, (1, 0, 2)), blocks)
    states = lax.all_to_all(packed, "mem", split_axis=0, concat_axis=0, tiled=True)

    lists = reading_pointers[0, 0]
    length = lists.shape[1]
    starts = jnp.min(lists, axis=1)
    all_starts = lax.all_gather(starts, "mem", axis=0, tiled=True)
    own_runs = sensor_space_runs[:, 0]
    before, after = from_neighbours(own_runs, HW)
    windows = cut_windows(all_starts, before, own_runs, after, length)
    windows = lax.all_to_all(windows, "mem", split_axis=0, concat_axis=0, tiled=True)
    lines = windows.reshape(blocks, groups, runs, length).transpose(1, 0, 2, 3)
    lines = lines.reshape(groups, members, length)

    statistics = jnp.concatenate([sensor_readings, noise_precision])
    stats_before, stats_after = from_neighbours(statistics, HW)
    statistics = jnp.concatenate([stats_before, statistics, stats_after], axis=1)
    moments = jnp.stack(
        [lax.dynamic_slice_in_dim(statistics, starts[g], length, axis=1) for g in range(groups)]
    )
    places = jnp.arange(length, dtype=jnp.int32)
    used = places[None, :] < reading_tally[0, 0][:, None]
    active = jnp.any(
        ((lists - starts[:, None])[:, :, None] == places[None, None, :]) & used[:, :, None], axis=1
    )
    weight = moments[:, 1] * active.astype(jnp.float32)
    turned = jax.vmap(local_transform)(lines, moments[:, 0], weight)
    transform = turned.transpose(1, 0, 2).reshape(members, groups * members)
    transform, states = lax.optimization_barrier((transform, states))
    analysed = analyse(transform, states, fields, columns, patch, groups)
    return jnp.transpose(analysed, (1, 0, 2))


def solution(mesh):
    placed = (
        P("mem", None, "reg"),
        P("mem", "reg", None),
        P("reg", None),
        P("reg", None),
        P("reg", "mem", None, None),
        P("reg", "mem", None),
    )
    return jax.shard_map(
        per_device, mesh=mesh, in_specs=placed, out_specs=P("mem", None, "reg"), check_vma=False
    )
```

```python
import functools
import math

import jax
import jax.numpy as jnp
from jax import lax
from jax.experimental import pallas as pl
from jax.experimental.pallas import tpu as pltpu
from jax.sharding import PartitionSpec as P

NS_ITERS = 6
HW = 256
LANES = 128
CHUNKS = 4
VMEM_LIMIT = 60 * 1024 * 1024

inflation = 1.1
MESH = pl.DeviceIdType.MESH


def lane_part(shape, width):
    return lax.broadcasted_iota(jnp.int32, shape, len(shape) - 1) // width


def swap_lane_parts(pieces, width):
    parts = len(pieces)
    part = lane_part(pieces[0].shape, width)
    swapped = []
    for d in range(parts):
        result = pieces[d]
        for s in range(parts):
            if s != d:
                moved = pltpu.roll(pieces[s], (s - d) * width % LANES, 1)
                result = jnp.where(part == s, moved, result)
        swapped.append(result)
    return swapped


def chunk_bounds(rows):
    edges = [rows * i // CHUNKS for i in range(CHUNKS + 1)]
    return list(zip(edges[:-1], edges[1:]))


def apply_rows(transform_ref, states_ref, result_ref, first, last, patch, groups):
    blocks, _, runs, _ = states_ref.shape
    members = blocks * runs

    def one(r):
        x = jnp.concatenate([states_ref[b, r] for b in range(blocks)], axis=0)
        x = x.astype(jnp.float32)
        center = jnp.sum(x, axis=0, keepdims=True) * (1.0 / members)
        pert = (x - center).astype(jnp.bfloat16).astype(jnp.float32)
        group = lane_part(pert.shape, patch) % groups
        masked = [jnp.where(group == g, pert, 0.0).astype(jnp.bfloat16) for g in range(groups)]
        return center, jnp.concatenate(masked, axis=0)

    def body(i, carry):
        r0 = first + 2 * i
        r1 = jnp.minimum(r0 + 1, last - 1)
        center0, masked0 = one(r0)
        center1, masked1 = one(r1)
        moved = jnp.dot(
            transform_ref[...],
            jnp.concatenate([masked0, masked1], axis=1),
            preferred_element_type=jnp.float32,
        )
        for r, center, lanes in ((r0, center0, slice(0, LANES)), (r1, center1, slice(LANES, None))):
            analysed = (moved[:, lanes] + center).astype(jnp.bfloat16)
            for b in range(blocks):
                result_ref[b, r] = analysed[b * runs : (b + 1) * runs]
        return carry

    lax.fori_loop(0, (last - first + 1) // 2, body, 0)


def unpack_row(received, result_ref, r, valid):
    blocks, rows, _, _ = received.shape
    columns = result_ref.shape[2]
    width = columns // blocks
    parts = LANES // width
    for tile in range(columns // LANES):
        lanes = slice(tile * LANES, (tile + 1) * LANES)
        pieces = [received[tile * parts + d, r].astype(jnp.float32) for d in range(parts)]
        swapped = swap_lane_parts(pieces, width)
        for s in range(valid):
            result_ref[s * rows + r, :, lanes] = swapped[s].astype(jnp.bfloat16)


def unpack_rows(received, result_ref, first, last):
    rows = received.shape[1]
    fields = result_ref.shape[0]
    parts = LANES // (result_ref.shape[2] // received.shape[0])
    whole = rows - (parts * rows - fields)

    def body(r, carry):
        unpack_row(received, result_ref, r, parts)
        return carry

    lax.fori_loop(first, min(last, whole), body, 0)
    for r in range(max(first, whole), last):
        unpack_row(received, result_ref, r, parts - 1)


def pack_rows(states_ref, packed, first, last):
    fields, _, columns = states_ref.shape
    blocks, rows, _, _ = packed.shape
    width = columns // blocks
    parts = LANES // width

    def body(r, carry):
        for tile in range(columns // LANES):
            lanes = slice(tile * LANES, (tile + 1) * LANES)
            pieces = [
                states_ref[jnp.minimum(s * rows + r, fields - 1), :, lanes].astype(jnp.float32)
                for s in range(parts)
            ]
            for d, piece in enumerate(swap_lane_parts(pieces, width)):
                packed[tile * parts + d, r] = piece.astype(jnp.bfloat16)
        return carry

    lax.fori_loop(first, last, body, 0)


def bit_of(start, bit, shape, kind):
    value = jnp.broadcast_to((start >> bit) & 1, shape)
    return value.astype(jnp.float32).astype(kind) > 0.5


def nearest_tiles(extended, start, length):
    shape = (extended.shape[0], LANES)
    keep = length // LANES
    total = extended.shape[1] // LANES
    tiles = [extended[:, i * LANES : (i + 1) * LANES] for i in range(total)]
    for bit in reversed(range((total - keep).bit_length())):
        shift = 1 << bit
        mask = bit_of(start, bit + LANES.bit_length() - 1, shape, extended.dtype)
        tiles = [
            jnp.where(mask, tiles[i + shift], tiles[i]) if i + shift < len(tiles) else tiles[i]
            for i in range(min(len(tiles), shift + keep))
        ]
    return tiles


def load_runs(extended, start, length):
    tiles = nearest_tiles(extended, start, length)
    count = extended.shape[0]
    shape = (2 * LANES, LANES)
    row = lax.broadcasted_iota(jnp.int32, shape, 0)
    lane = lax.broadcasted_iota(jnp.int32, shape, 1)
    chosen = (row - lane == jnp.broadcast_to(start & (LANES - 1), shape)).astype(jnp.float32)
    pairs = [jnp.concatenate([a, b], axis=1) for a, b in zip(tiles[:-1], tiles[1:])]
    shifted = dot(jnp.concatenate(pairs, axis=0), chosen.astype(jnp.bfloat16))
    shifted = shifted.astype(jnp.bfloat16)
    return jnp.concatenate(
        [shifted[i * count : (i + 1) * count] for i in range(len(pairs))], axis=1
    )


def load_statistics(extended, start, length):
    tiles = nearest_tiles(extended, start, length)
    shape = tiles[0].shape
    for bit in range(LANES.bit_length() - 1):
        mask = bit_of(start, bit, shape, jnp.float32)
        tiles = [jnp.where(mask, pltpu.roll(t, LANES - (1 << bit), 1), t) for t in tiles]
    lane = lax.broadcasted_iota(jnp.int32, shape, 1)
    here = lane < LANES - jnp.broadcast_to(start & (LANES - 1), shape)
    return jnp.concatenate(
        [jnp.where(here, a, b) for a, b in zip(tiles[:-1], tiles[1:])], axis=1
    )


def split(x, terms):
    pieces = []
    for _ in range(terms):
        piece = x.astype(jnp.bfloat16)
        pieces.append(piece)
        x = x - piece.astype(jnp.float32)
    return pieces


def dot(a, b):
    return jnp.dot(a, b, preferred_element_type=jnp.float32)


def dot_lanes(a, b):
    return lax.dot_general(a, b, (((1,), (1,)), ((), ())), preferred_element_type=jnp.float32)


def dot_narrow(a, b):
    (a0, a1), (b0, b1) = split(a, 2), split(b, 2)
    return dot(a0, b0) + (dot(a0, b1) + dot(a1, b0))


def build_transform(lines, moments, active, transform, g, iterate, root, factor):
    blocks, _, runs, _ = lines.shape
    members = blocks * runs
    observed = jnp.concatenate([lines[b, g] for b in range(blocks)], axis=0).astype(jnp.float32)
    ens_mean = jnp.sum(observed, axis=0, keepdims=True) * (1.0 / members)
    anomaly = (observed - ens_mean).astype(jnp.bfloat16)
    weight = moments[1:2] * active
    rows = lax.broadcasted_iota(jnp.int32, (members, members), 0)
    lanes = lax.broadcasted_iota(jnp.int32, (members, members), 1)
    identity = (rows == lanes).astype(jnp.float32)
    weighted = split(anomaly.astype(jnp.float32) * weight, 2)
    gram = dot_lanes(anomaly, weighted[0]) + dot_lanes(anomaly, weighted[1])
    gram = gram + (members - 1) / inflation * identity
    innovation = jnp.broadcast_to(weight * (moments[0:1] - ens_mean), (16, weight.shape[1]))
    innovation = split(innovation, 3)
    innovation_sum = sum(dot_lanes(piece, anomaly) for piece in innovation)[0:1]
    squares = jnp.sum(jnp.sum(gram * gram, axis=0, keepdims=True), axis=1, keepdims=True)
    frobenius = jnp.sqrt(squares)
    iterate[...] = gram / frobenius
    factor[...] = 1.5 * identity - 0.5 * iterate[...]
    root[...] = factor[...]

    def step(i, carry):
        iterate[...] = dot_narrow(iterate[...], factor[...])
        factor[...] = 1.5 * identity - 0.5 * dot_narrow(root[...], iterate[...])
        root[...] = dot_narrow(factor[...], root[...])
        return carry

    lax.fori_loop(1, NS_ITERS, step, 0)
    inverse_root = root[...] / jnp.sqrt(frobenius)
    inner = jnp.sum(inverse_root * innovation_sum, axis=1, keepdims=True)
    mean_weight = jnp.sum(inverse_root * inner, axis=0, keepdims=True)
    turned = math.sqrt(members - 1) * inverse_root + mean_weight
    transform[g] = turned.astype(jnp.bfloat16)


def kernel(
    patch,
    groups,
    states_ref,
    runs_ref,
    stats_ref,
    starts_ref,
    active_ref,
    result_ref,
    packed,
    arrived,
    outgoing,
    received,
    extended,
    stats,
    all_starts,
    windows,
    lines,
    transform,
    joined,
    iterate,
    root,
    factor,
    send_sem,
    recv_sem,
    small_send,
    small_recv,
    halo_send,
    halo_recv,
):
    blocks, rows, _, _ = packed.shape
    length = lines.shape[3]
    own = runs_ref.shape[1]
    me = lax.axis_index("mem")
    region = lax.axis_index("reg")
    regions = lax.axis_size("reg")
    after = {"reg": lax.rem(region + 1, regions)}
    before = {"reg": lax.rem(region + regions - 1, regions)}
    peers = [lax.rem(me + k, blocks) for k in range(1, blocks)]

    def send(source, target, sems, device):
        copy = pltpu.make_async_remote_copy(
            src_ref=source,
            dst_ref=target,
            send_sem=sems[0],
            recv_sem=sems[1],
            device_id=device,
            device_id_type=MESH,
        )
        copy.start()
        return copy

    barrier = pltpu.get_barrier_semaphore()
    for device in [{"mem": peer} for peer in peers] + [after, before]:
        pl.semaphore_signal(barrier, inc=1, device_id=device, device_id_type=MESH)
    pl.semaphore_wait(barrier, blocks + 1)

    small = []
    for k, peer in enumerate(peers):
        sems = small_send.at[0, k], small_recv.at[0, k]
        small.append(send(starts_ref, all_starts.at[me], sems, {"mem": peer}))
    last_columns, first_columns = pl.ds(own - HW, HW), pl.ds(0, HW)
    beyond = pl.ds(own + HW, HW)
    for i, (source, target) in enumerate(((runs_ref, extended), (stats_ref, stats))):
        sems = halo_send.at[2 * i], halo_recv.at[2 * i]
        small.append(
            send(source.at[:, last_columns], target.at[:, first_columns], sems, after)
        )
        sems = halo_send.at[2 * i + 1], halo_recv.at[2 * i + 1]
        small.append(send(source.at[:, first_columns], target.at[:, beyond], sems, before))
    extended[:, HW : HW + own] = runs_ref[...]
    stats[:, HW : HW + own] = stats_ref[...]
    all_starts[me] = starts_ref[...]

    bounds = chunk_bounds(rows)
    forward = []

    def exchange_states(c):
        first, last = bounds[c]
        pack_rows(states_ref, packed, first, last)
        span = pl.ds(first, last - first)
        for k, peer in enumerate(peers):
            sems = send_sem.at[0, k, c], recv_sem.at[0, k, c]
            forward.append(
                send(packed.at[peer, span], arrived.at[me, span], sems, {"mem": peer})
            )
        arrived[me, span] = packed[me, span]

    exchange_states(0)
    for copy in small:
        copy.wait_recv()

    sent_windows = []
    for k, peer in enumerate(peers):

        def cut(g, carry, peer=peer):
            windows[peer, g] = load_runs(extended, all_starts[peer, pl.ds(g, 1), :], length)
            return carry

        lax.fori_loop(0, groups, cut, 0)
        sems = small_send.at[1, k], small_recv.at[1, k]
        sent_windows.append(send(windows.at[peer], lines.at[me], sems, {"mem": peer}))

    def cut_own(g, carry):
        lines[me, g] = load_runs(extended, starts_ref[pl.ds(g, 1), :], length)
        return carry

    lax.fori_loop(0, groups, cut_own, 0)
    for c in range(1, CHUNKS):
        exchange_states(c)
    for copy in sent_windows:
        copy.wait_recv()

    def build(g, carry):
        moments = load_statistics(stats, starts_ref[pl.ds(g, 1), :], length)
        active = active_ref[pl.ds(g, 1), :]
        build_transform(lines, moments, active, transform, g, iterate, root, factor)
        return carry

    lax.fori_loop(0, groups, build, 0)
    members = joined.shape[0]
    for g in range(groups):
        joined[:, g * members : (g + 1) * members] = transform[g]

    returned = []
    for c, (first, last) in enumerate(bounds):
        for copy in forward[c * (blocks - 1) : (c + 1) * (blocks - 1)]:
            copy.wait_recv()
        apply_rows(joined, arrived, outgoing, first, last, patch, groups)
        span = pl.ds(first, last - first)
        for k, peer in enumerate(peers):
            sems = send_sem.at[1, k, c], recv_sem.at[1, k, c]
            returned.append(
                send(outgoing.at[peer, span], received.at[me, span], sems, {"mem": peer})
            )
        received[me, span] = outgoing[me, span]
    for c, (first, last) in enumerate(bounds):
        for copy in returned[c * (blocks - 1) : (c + 1) * (blocks - 1)]:
            copy.wait_recv()
        unpack_rows(received, result_ref, first, last)
    for copy in small + sent_windows + forward + returned:
        copy.wait_send()


def assimilate(states, runs, statistics, starts, active, blocks, groups):
    fields, count, columns = states.shape
    members = count * blocks
    length = active.shape[1]
    own = runs.shape[1]
    width = columns // blocks
    rows = -(-fields // (LANES // width))
    packed = pltpu.VMEM((blocks, rows, count, LANES), jnp.bfloat16)
    square = pltpu.VMEM((members, members), jnp.float32)
    window = pltpu.VMEM((blocks, groups, count, length), jnp.bfloat16)
    dma = pltpu.SemaphoreType.DMA
    return pl.pallas_call(
        functools.partial(kernel, width // groups, groups),
        out_shape=jax.ShapeDtypeStruct(states.shape, jnp.bfloat16),
        in_specs=[pl.BlockSpec(memory_space=pltpu.VMEM)] * 5,
        out_specs=pl.BlockSpec(memory_space=pltpu.VMEM),
        scratch_shapes=[
            packed,
            packed,
            packed,
            packed,
            pltpu.VMEM((count, own + 2 * HW), jnp.bfloat16),
            pltpu.VMEM((statistics.shape[0], own + 2 * HW), jnp.float32),
            pltpu.VMEM((blocks,) + starts.shape, jnp.int32),
            window,
            window,
            pltpu.VMEM((groups, members, members), jnp.bfloat16),
            pltpu.VMEM((members, groups * members), jnp.bfloat16),
            square,
            square,
            square,
            dma((2, blocks - 1, CHUNKS)),
            dma((2, blocks - 1, CHUNKS)),
            dma((2, blocks - 1)),
            dma((2, blocks - 1)),
            dma((4,)),
            dma((4,)),
        ],
        compiler_params=pltpu.CompilerParams(
            collective_id=0, has_side_effects=True, vmem_limit_bytes=VMEM_LIMIT
        ),
        name="assimilate",
    )(states, runs, statistics, starts, active)


def per_device(
    prior_states,
    sensor_space_runs,
    sensor_readings,
    noise_precision,
    reading_pointers,
    reading_tally,
):
    blocks = lax.axis_size("mem")
    groups = reading_tally.shape[2]
    lists = reading_pointers[0, 0]
    length = lists.shape[1]
    starts = jnp.min(lists, axis=1)
    places = jnp.arange(length, dtype=jnp.int32)
    used = places[None, :] < reading_tally[0, 0][:, None]
    active = jnp.any(
        ((lists - starts[:, None])[:, :, None] == places[None, None, :]) & used[:, :, None], axis=1
    ).astype(jnp.float32)
    start_tile = jnp.broadcast_to(starts[:, None], (groups, LANES))
    start_tile = jnp.pad(start_tile, ((0, -groups % 8), (0, 0)))
    statistics = jnp.concatenate([sensor_readings, noise_precision])
    statistics = jnp.pad(statistics, ((0, 6), (0, 0)))
    analysed = assimilate(
        jnp.transpose(prior_states, (1, 0, 2)),
        sensor_space_runs[:, 0],
        statistics,
        start_tile,
        active,
        blocks,
        groups,
    )
    return jnp.transpose(analysed, (1, 0, 2))


def solution(mesh):
    placed = (
        P("mem", None, "reg"),
        P("mem", "reg", None),
        P("reg", None),
        P("reg", None),
        P("reg", "mem", None, None),
        P("reg", "mem", None),
    )
    return jax.shard_map(
        per_device, mesh=mesh, in_specs=placed, out_specs=P("mem", None, "reg"), check_vma=False
    )
```

```python
import functools
import math

import jax
import jax.numpy as jnp
from jax import lax
from jax.experimental import pallas as pl
from jax.experimental.pallas import tpu as pltpu
from jax.sharding import PartitionSpec as P

NS_ITERS = 6
HW = 256
LANES = 128
CHUNKS = 8
VMEM_LIMIT = 48 * 1024 * 1024

inflation = 1.1
MESH = pl.DeviceIdType.MESH


def lane_part(shape, width):
    return lax.broadcasted_iota(jnp.int32, shape, len(shape) - 1) // width


def swap_lane_parts(pieces, width):
    parts = len(pieces)
    part = lane_part(pieces[0].shape, width)
    swapped = []
    for d in range(parts):
        result = pieces[d]
        for s in range(parts):
            if s != d:
                moved = pltpu.roll(pieces[s], (s - d) * width % LANES, 1)
                result = jnp.where(part == s, moved, result)
        swapped.append(result)
    return swapped


def chunk_bounds(rows):
    edges = [rows * i // CHUNKS // 2 * 2 for i in range(CHUNKS)] + [rows]
    return list(zip(edges[:-1], edges[1:]))


def apply_rows(transform_ref, states_ref, result_ref, first, last, patch, groups):
    blocks, _, runs, _ = states_ref.shape
    members = blocks * runs

    def one(r):
        x = jnp.concatenate([states_ref[b, r] for b in range(blocks)], axis=0)
        x = x.astype(jnp.float32)
        center = jnp.sum(x, axis=0, keepdims=True) * (1.0 / members)
        pert = (x - center).astype(jnp.bfloat16).astype(jnp.float32)
        group = lane_part(pert.shape, patch) % groups
        masked = [jnp.where(group == g, pert, 0.0).astype(jnp.bfloat16) for g in range(groups)]
        return center, jnp.concatenate(masked, axis=0)

    def body(i, carry):
        r0 = first + 2 * i
        r1 = jnp.minimum(r0 + 1, last - 1)
        center0, masked0 = one(r0)
        center1, masked1 = one(r1)
        moved = jnp.dot(
            transform_ref[...],
            jnp.concatenate([masked0, masked1], axis=1),
            preferred_element_type=jnp.float32,
        )
        for r, center, lanes in ((r0, center0, slice(0, LANES)), (r1, center1, slice(LANES, None))):
            analysed = (moved[:, lanes] + center).astype(jnp.bfloat16)
            for b in range(blocks):
                result_ref[b, r] = analysed[b * runs : (b + 1) * runs]
        return carry

    lax.fori_loop(0, (last - first + 1) // 2, body, 0)


def unpack_row(received, result_ref, r, valid):
    blocks, rows, _, _ = received.shape
    columns = result_ref.shape[2]
    width = columns // blocks
    parts = LANES // width
    for tile in range(columns // LANES):
        lanes = slice(tile * LANES, (tile + 1) * LANES)
        pieces = [received[tile * parts + d, r].astype(jnp.float32) for d in range(parts)]
        swapped = swap_lane_parts(pieces, width)
        for s in range(valid):
            result_ref[s * rows + r, :, lanes] = swapped[s].astype(jnp.bfloat16)


def unpack_rows(received, result_ref, first, last):
    rows = received.shape[1]
    fields = result_ref.shape[0]
    parts = LANES // (result_ref.shape[2] // received.shape[0])
    whole = rows - (parts * rows - fields)

    def body(r, carry):
        unpack_row(received, result_ref, r, parts)
        return carry

    lax.fori_loop(first, min(last, whole), body, 0)
    for r in range(max(first, whole), last):
        unpack_row(received, result_ref, r, parts - 1)


def pack_rows(states_ref, packed, first, last):
    fields, _, columns = states_ref.shape
    blocks, rows, _, _ = packed.shape
    width = columns // blocks
    parts = LANES // width

    def body(r, carry):
        for tile in range(columns // LANES):
            lanes = slice(tile * LANES, (tile + 1) * LANES)
            pieces = [
                states_ref[jnp.minimum(s * rows + r, fields - 1), :, lanes].astype(jnp.float32)
                for s in range(parts)
            ]
            for d, piece in enumerate(swap_lane_parts(pieces, width)):
                packed[tile * parts + d, r] = piece.astype(jnp.bfloat16)
        return carry

    lax.fori_loop(first, last, body, 0)


def bit_of(start, bit, shape, kind):
    value = jnp.broadcast_to((start >> bit) & 1, shape)
    return value.astype(jnp.float32).astype(kind) > 0.5


def nearest_tiles(extended, start, length):
    shape = (extended.shape[0], LANES)
    keep = length // LANES
    total = extended.shape[1] // LANES
    tiles = [extended[:, i * LANES : (i + 1) * LANES] for i in range(total)]
    for bit in reversed(range((total - keep).bit_length())):
        shift = 1 << bit
        mask = bit_of(start, bit + LANES.bit_length() - 1, shape, extended.dtype)
        tiles = [
            jnp.where(mask, tiles[i + shift], tiles[i]) if i + shift < len(tiles) else tiles[i]
            for i in range(min(len(tiles), shift + keep))
        ]
    return tiles


def load_runs(extended, start, length):
    tiles = nearest_tiles(extended, start, length)
    count = extended.shape[0]
    shape = (2 * LANES, LANES)
    row = lax.broadcasted_iota(jnp.int32, shape, 0)
    lane = lax.broadcasted_iota(jnp.int32, shape, 1)
    chosen = (row - lane == jnp.broadcast_to(start & (LANES - 1), shape)).astype(jnp.float32)
    pairs = [jnp.concatenate([a, b], axis=1) for a, b in zip(tiles[:-1], tiles[1:])]
    shifted = dot(jnp.concatenate(pairs, axis=0), chosen.astype(jnp.bfloat16))
    shifted = shifted.astype(jnp.bfloat16)
    return jnp.concatenate(
        [shifted[i * count : (i + 1) * count] for i in range(len(pairs))], axis=1
    )


def load_statistics(extended, start, length):
    tiles = nearest_tiles(extended, start, length)
    shape = tiles[0].shape
    for bit in range(LANES.bit_length() - 1):
        mask = bit_of(start, bit, shape, jnp.float32)
        tiles = [jnp.where(mask, pltpu.roll(t, LANES - (1 << bit), 1), t) for t in tiles]
    lane = lax.broadcasted_iota(jnp.int32, shape, 1)
    here = lane < LANES - jnp.broadcast_to(start & (LANES - 1), shape)
    return jnp.concatenate(
        [jnp.where(here, a, b) for a, b in zip(tiles[:-1], tiles[1:])], axis=1
    )


def split(x, terms):
    pieces = []
    for _ in range(terms):
        piece = x.astype(jnp.bfloat16)
        pieces.append(piece)
        x = x - piece.astype(jnp.float32)
    return pieces


def dot(a, b):
    return jnp.dot(a, b, preferred_element_type=jnp.float32)


def dot_lanes(a, b):
    return lax.dot_general(a, b, (((1,), (1,)), ((), ())), preferred_element_type=jnp.float32)


def dot_narrow(a, b):
    return dot(a[0], b[0]) + (dot(a[0], b[1]) + dot(a[1], b[0]))


def used_positions(lists_ref, tally_ref, start, g):
    length = lists_ref.shape[1]
    shape = (length, length)
    tallies = tally_ref[...].astype(jnp.float32)
    lane = lax.broadcasted_iota(jnp.int32, tallies.shape, 1)
    tally = jnp.sum(jnp.where(lane == g, tallies, 0.0), axis=1, keepdims=True)
    place = lists_ref[pl.ds(g, 1), :] - jnp.concatenate([start] * (length // LANES), axis=1)
    listed = lax.broadcasted_iota(jnp.int32, shape, 0) == jnp.broadcast_to(place, shape)
    listed = listed.astype(jnp.float32).astype(jnp.bfloat16)
    entry = lax.broadcasted_iota(jnp.int32, (16, length), 1).astype(jnp.float32)
    used = (entry < tally).astype(jnp.float32).astype(jnp.bfloat16)
    return dot_lanes(used, listed)[0:1]


def identity_of(members):
    rows = lax.broadcasted_iota(jnp.int32, (members, members), 0)
    lanes = lax.broadcasted_iota(jnp.int32, (members, members), 1)
    return (rows == lanes).astype(jnp.float32)


def begin_root(lines, readings, weight, g, iterate, root, factor, innovation_sum, norm):
    blocks, _, runs, _ = lines.shape
    members = blocks * runs
    observed = jnp.concatenate([lines[b, g] for b in range(blocks)], axis=0).astype(jnp.float32)
    ens_mean = jnp.sum(observed, axis=0, keepdims=True) * (1.0 / members)
    anomaly = (observed - ens_mean).astype(jnp.bfloat16)
    identity = identity_of(members)
    weighted = split(anomaly.astype(jnp.float32) * weight, 2)
    gram = dot_lanes(anomaly, weighted[0]) + dot_lanes(anomaly, weighted[1])
    gram = gram + (members - 1) / inflation * identity
    innovation = jnp.broadcast_to(weight * (readings - ens_mean), (16, weight.shape[1]))
    innovation = split(innovation, 3)
    innovation_sum[g] = sum(dot_lanes(piece, anomaly) for piece in innovation)[0:8]
    squares = jnp.sum(jnp.sum(gram * gram, axis=0, keepdims=True), axis=1, keepdims=True)
    frobenius = jnp.sqrt(squares)
    norm[g] = jnp.broadcast_to(jnp.sqrt(frobenius), norm.shape[1:])
    scaled = gram / frobenius
    first = 1.5 * identity - 0.5 * scaled
    keep(iterate, g, scaled)
    keep(factor, g, first)
    keep(root, g, first)


def keep(ref, g, value):
    ref[g, 0], ref[g, 1] = split(value, 2)


def refine_roots(iterate, root, factor):
    groups, _, members, _ = iterate.shape

    def step(i, carry):
        for g in range(groups):
            keep(iterate, g, dot_narrow(iterate[g], factor[g]))
        for g in range(groups):
            product = dot_narrow(root[g], iterate[g])
            keep(factor, g, 1.5 * identity_of(members) - 0.5 * product)
        for g in range(groups):
            keep(root, g, dot_narrow(factor[g], root[g]))
        return carry

    lax.fori_loop(1, NS_ITERS, step, 0)


def finish_transform(root, innovation_sum, norm, joined, g):
    members = root.shape[2]
    inverse_root = root[g, 0].astype(jnp.float32) + root[g, 1].astype(jnp.float32)
    inverse_root = inverse_root * (1.0 / norm[g][0:1, 0:1])
    inner = jnp.sum(inverse_root * innovation_sum[g][0:1], axis=1, keepdims=True)
    mean_weight = jnp.sum(inverse_root * inner, axis=0, keepdims=True)
    turned = math.sqrt(members - 1) * inverse_root + mean_weight
    joined[:, g * members : (g + 1) * members] = turned.astype(jnp.bfloat16)


def kernel(
    patch,
    groups,
    states_ref,
    runs_ref,
    readings_ref,
    precision_ref,
    lists_ref,
    tally_ref,
    result_ref,
    packed,
    arrived,
    outgoing,
    received,
    extended,
    readings,
    precision,
    starts,
    all_starts,
    windows,
    lines,
    joined,
    iterate,
    root,
    factor,
    innovation_sum,
    norm,
    send_sem,
    recv_sem,
    small_send,
    small_recv,
    halo_send,
    halo_recv,
):
    blocks, rows, _, _ = packed.shape
    length = lines.shape[3]
    own = runs_ref.shape[1]
    me = lax.axis_index("mem")
    region = lax.axis_index("reg")
    regions = lax.axis_size("reg")
    after = {"reg": lax.rem(region + 1, regions)}
    before = {"reg": lax.rem(region + regions - 1, regions)}
    peers = [lax.rem(me + k, blocks) for k in range(1, blocks)]

    def send(source, target, sems, device):
        copy = pltpu.make_async_remote_copy(
            src_ref=source,
            dst_ref=target,
            send_sem=sems[0],
            recv_sem=sems[1],
            device_id=device,
            device_id_type=MESH,
        )
        copy.start()
        return copy

    lowest = jnp.min(lists_ref[...].astype(jnp.float32), axis=1, keepdims=True)
    starts[...] = jnp.zeros_like(starts)
    starts[0:groups, :] = jnp.broadcast_to(lowest, (groups, LANES)).astype(jnp.int32)

    barrier = pltpu.get_barrier_semaphore()
    for device in [{"mem": peer} for peer in peers] + [after, before]:
        pl.semaphore_signal(barrier, inc=1, device_id=device, device_id_type=MESH)
    pl.semaphore_wait(barrier, blocks + 1)

    small = []
    for k, peer in enumerate(peers):
        sems = small_send.at[0, k], small_recv.at[0, k]
        small.append(send(starts, all_starts.at[me], sems, {"mem": peer}))
    last_columns, first_columns = pl.ds(own - HW, HW), pl.ds(0, HW)
    beyond = pl.ds(own + HW, HW)
    for i, (source, target) in enumerate(
        ((runs_ref, extended), (readings_ref, readings), (precision_ref, precision))
    ):
        sems = halo_send.at[2 * i], halo_recv.at[2 * i]
        small.append(
            send(source.at[:, last_columns], target.at[:, first_columns], sems, after)
        )
        sems = halo_send.at[2 * i + 1], halo_recv.at[2 * i + 1]
        small.append(send(source.at[:, first_columns], target.at[:, beyond], sems, before))
    extended[:, HW : HW + own] = runs_ref[...]
    readings[:, HW : HW + own] = readings_ref[...]
    precision[:, HW : HW + own] = precision_ref[...]

    bounds = chunk_bounds(rows)
    forward = []

    def exchange_states(c):
        first, last = bounds[c]
        pack_rows(states_ref, packed, first, last)
        span = pl.ds(first, last - first)
        for k, peer in enumerate(peers):
            sems = send_sem.at[0, k, c], recv_sem.at[0, k, c]
            forward.append(
                send(packed.at[peer, span], arrived.at[me, span], sems, {"mem": peer})
            )
        arrived[me, span] = packed[me, span]

    exchange_states(0)
    for copy in small:
        copy.wait_recv()

    sent_windows = []
    for k, peer in enumerate(peers):

        def cut(g, carry, peer=peer):
            windows[peer, g] = load_runs(extended, all_starts[peer, pl.ds(g, 1), :], length)
            return carry

        lax.fori_loop(0, groups, cut, 0)
        sems = small_send.at[1, k], small_recv.at[1, k]
        sent_windows.append(send(windows.at[peer], lines.at[me], sems, {"mem": peer}))

    def cut_own(g, carry):
        lines[me, g] = load_runs(extended, starts[pl.ds(g, 1), :], length)
        return carry

    lax.fori_loop(0, groups, cut_own, 0)
    for c in range(1, CHUNKS):
        exchange_states(c)
    for copy in sent_windows:
        copy.wait_recv()

    def begin(g, carry):
        start = starts[pl.ds(g, 1), :]
        weight = load_statistics(precision, start, length)
        weight = weight * used_positions(lists_ref, tally_ref, start, g)
        observed = load_statistics(readings, start, length)
        begin_root(lines, observed, weight, g, iterate, root, factor, innovation_sum, norm)
        return carry

    lax.fori_loop(0, groups, begin, 0)
    refine_roots(iterate, root, factor)
    for g in range(groups):
        finish_transform(root, innovation_sum, norm, joined, g)

    returned = []
    for c, (first, last) in enumerate(bounds):
        for copy in forward[c * (blocks - 1) : (c + 1) * (blocks - 1)]:
            copy.wait_recv()
        apply_rows(joined, arrived, outgoing, first, last, patch, groups)
        span = pl.ds(first, last - first)
        for k, peer in enumerate(peers):
            sems = send_sem.at[1, k, c], recv_sem.at[1, k, c]
            returned.append(
                send(outgoing.at[peer, span], received.at[me, span], sems, {"mem": peer})
            )
        received[me, span] = outgoing[me, span]
    for c, (first, last) in enumerate(bounds):
        for copy in returned[c * (blocks - 1) : (c + 1) * (blocks - 1)]:
            copy.wait_recv()
        unpack_rows(received, result_ref, first, last)
    for copy in small + sent_windows + forward + returned:
        copy.wait_send()


def assimilate(states, runs, readings, precision, lists, tally, blocks):
    fields, count, columns = states.shape
    groups, length = lists.shape
    members = count * blocks
    own = runs.shape[1]
    width = columns // blocks
    rows = -(-fields // (LANES // width))
    packed = pltpu.VMEM((blocks, rows, count, LANES), jnp.bfloat16)
    square = pltpu.VMEM((groups, 2, members, members), jnp.bfloat16)
    window = pltpu.VMEM((blocks, groups, count, length), jnp.bfloat16)
    start_rows = groups + -groups % 8
    dma = pltpu.SemaphoreType.DMA
    return pl.pallas_call(
        functools.partial(kernel, width // groups, groups),
        out_shape=pltpu.VMEM(states.shape, jnp.bfloat16),
        in_specs=[pl.BlockSpec(memory_space=pltpu.VMEM)] * 6,
        out_specs=pl.BlockSpec(memory_space=pltpu.VMEM),
        scratch_shapes=[
            packed,
            packed,
            packed,
            packed,
            pltpu.VMEM((count, own + 2 * HW), jnp.bfloat16),
            pltpu.VMEM((1, own + 2 * HW), jnp.float32),
            pltpu.VMEM((1, own + 2 * HW), jnp.float32),
            pltpu.VMEM((start_rows, LANES), jnp.int32),
            pltpu.VMEM((blocks, start_rows, LANES), jnp.int32),
            window,
            window,
            pltpu.VMEM((members, groups * members), jnp.bfloat16),
            square,
            square,
            square,
            pltpu.VMEM((groups, 8, members), jnp.float32),
            pltpu.VMEM((groups, 8, LANES), jnp.float32),
            dma((2, blocks - 1, CHUNKS)),
            dma((2, blocks - 1, CHUNKS)),
            dma((2, blocks - 1)),
            dma((2, blocks - 1)),
            dma((6,)),
            dma((6,)),
        ],
        compiler_params=pltpu.CompilerParams(
            collective_id=0, has_side_effects=True, vmem_limit_bytes=VMEM_LIMIT
        ),
        name="assimilate",
    )(states, runs, readings, precision, lists, tally)


def per_device(
    prior_states,
    sensor_space_runs,
    sensor_readings,
    noise_precision,
    reading_pointers,
    reading_tally,
):
    analysed = assimilate(
        jnp.transpose(prior_states, (1, 0, 2)),
        sensor_space_runs[:, 0],
        sensor_readings,
        noise_precision,
        reading_pointers[0, 0],
        reading_tally[0],
        lax.axis_size("mem"),
    )
    return jnp.transpose(analysed, (1, 0, 2))


def solution(mesh):
    placed = (
        P("mem", None, "reg"),
        P("mem", "reg", None),
        P("reg", None),
        P("reg", None),
        P("reg", "mem", None, None),
        P("reg", "mem", None),
    )
    return jax.shard_map(
        per_device, mesh=mesh, in_specs=placed, out_specs=P("mem", None, "reg"), check_vma=False
    )
```

```python
import functools
import math

import jax
import jax.numpy as jnp
from jax import lax
from jax.experimental import pallas as pl
from jax.experimental.pallas import tpu as pltpu
from jax.sharding import PartitionSpec as P

NS_ITERS = 6
HW = 256
LANES = 128
CHUNKS = 8
VMEM_LIMIT = 48 * 1024 * 1024

inflation = 1.1
MESH = pl.DeviceIdType.MESH


def lane_part(shape, width):
    return lax.broadcasted_iota(jnp.int32, shape, len(shape) - 1) // width


def swap_lane_parts(pieces, width):
    parts = len(pieces)
    part = lane_part(pieces[0].shape, width)
    swapped = []
    for d in range(parts):
        result = pieces[d]
        for s in range(parts):
            if s != d:
                moved = pltpu.roll(pieces[s], (s - d) * width % LANES, 1)
                result = jnp.where(part == s, moved, result)
        swapped.append(result)
    return swapped


def chunk_bounds(rows):
    edges = [rows * i // CHUNKS // 2 * 2 for i in range(CHUNKS)] + [rows]
    return list(zip(edges[:-1], edges[1:]))


def apply_rows(transform_ref, states_ref, result_ref, first, last, patch, groups):
    blocks, _, runs, _ = states_ref.shape
    members = blocks * runs

    def one(r):
        x = jnp.concatenate([states_ref[b, r] for b in range(blocks)], axis=0)
        x = x.astype(jnp.float32)
        center = jnp.sum(x, axis=0, keepdims=True) * (1.0 / members)
        pert = (x - center).astype(jnp.bfloat16).astype(jnp.float32)
        group = lane_part(pert.shape, patch) % groups
        masked = [jnp.where(group == g, pert, 0.0).astype(jnp.bfloat16) for g in range(groups)]
        return center, jnp.concatenate(masked, axis=0)

    def body(i, carry):
        r0 = first + 2 * i
        r1 = jnp.minimum(r0 + 1, last - 1)
        center0, masked0 = one(r0)
        center1, masked1 = one(r1)
        moved = jnp.dot(
            transform_ref[...],
            jnp.concatenate([masked0, masked1], axis=1),
            preferred_element_type=jnp.float32,
        )
        for r, center, lanes in ((r0, center0, slice(0, LANES)), (r1, center1, slice(LANES, None))):
            analysed = (moved[:, lanes] + center).astype(jnp.bfloat16)
            for b in range(blocks):
                result_ref[b, r] = analysed[b * runs : (b + 1) * runs]
        return carry

    lax.fori_loop(0, (last - first + 1) // 2, body, 0)


def unpack_row(received, result_ref, r, valid):
    blocks, rows, _, _ = received.shape
    columns = result_ref.shape[2]
    width = columns // blocks
    parts = LANES // width
    for tile in range(columns // LANES):
        lanes = slice(tile * LANES, (tile + 1) * LANES)
        pieces = [received[tile * parts + d, r].astype(jnp.float32) for d in range(parts)]
        swapped = swap_lane_parts(pieces, width)
        for s in range(valid):
            result_ref[s * rows + r, :, lanes] = swapped[s].astype(jnp.bfloat16)


def unpack_rows(received, result_ref, first, last):
    rows = received.shape[1]
    fields = result_ref.shape[0]
    parts = LANES // (result_ref.shape[2] // received.shape[0])
    whole = rows - (parts * rows - fields)

    def body(r, carry):
        unpack_row(received, result_ref, r, parts)
        return carry

    lax.fori_loop(first, min(last, whole), body, 0)
    for r in range(max(first, whole), last):
        unpack_row(received, result_ref, r, parts - 1)


def pack_rows(states_ref, packed, first, last):
    fields, _, columns = states_ref.shape
    blocks, rows, _, _ = packed.shape
    width = columns // blocks
    parts = LANES // width

    def body(r, carry):
        for tile in range(columns // LANES):
            lanes = slice(tile * LANES, (tile + 1) * LANES)
            pieces = [
                states_ref[jnp.minimum(s * rows + r, fields - 1), :, lanes].astype(jnp.float32)
                for s in range(parts)
            ]
            for d, piece in enumerate(swap_lane_parts(pieces, width)):
                packed[tile * parts + d, r] = piece.astype(jnp.bfloat16)
        return carry

    lax.fori_loop(first, last, body, 0)


def bit_of(start, bit, shape, kind):
    value = jnp.broadcast_to((start >> bit) & 1, shape)
    return value.astype(jnp.float32).astype(kind) > 0.5


def nearest_tiles(extended, start, length):
    shape = (extended.shape[0], LANES)
    keep = length // LANES
    total = extended.shape[1] // LANES
    tiles = [extended[:, i * LANES : (i + 1) * LANES] for i in range(total)]
    for bit in reversed(range((total - keep).bit_length())):
        shift = 1 << bit
        mask = bit_of(start, bit + LANES.bit_length() - 1, shape, extended.dtype)
        tiles = [
            jnp.where(mask, tiles[i + shift], tiles[i]) if i + shift < len(tiles) else tiles[i]
            for i in range(min(len(tiles), shift + keep))
        ]
    return tiles


def load_runs(extended, start, length):
    tiles = nearest_tiles(extended, start, length)
    count = extended.shape[0]
    shape = (2 * LANES, LANES)
    row = lax.broadcasted_iota(jnp.int32, shape, 0)
    lane = lax.broadcasted_iota(jnp.int32, shape, 1)
    chosen = (row - lane == jnp.broadcast_to(start & (LANES - 1), shape)).astype(jnp.float32)
    pairs = [jnp.concatenate([a, b], axis=1) for a, b in zip(tiles[:-1], tiles[1:])]
    shifted = dot(jnp.concatenate(pairs, axis=0), chosen.astype(jnp.bfloat16))
    shifted = shifted.astype(jnp.bfloat16)
    return jnp.concatenate(
        [shifted[i * count : (i + 1) * count] for i in range(len(pairs))], axis=1
    )


def load_statistics(extended, start, length):
    tiles = nearest_tiles(extended, start, length)
    shape = tiles[0].shape
    for bit in range(LANES.bit_length() - 1):
        mask = bit_of(start, bit, shape, jnp.float32)
        tiles = [jnp.where(mask, pltpu.roll(t, LANES - (1 << bit), 1), t) for t in tiles]
    lane = lax.broadcasted_iota(jnp.int32, shape, 1)
    here = lane < LANES - jnp.broadcast_to(start & (LANES - 1), shape)
    return jnp.concatenate(
        [jnp.where(here, a, b) for a, b in zip(tiles[:-1], tiles[1:])], axis=1
    )


def split(x, terms):
    pieces = []
    for _ in range(terms):
        piece = x.astype(jnp.bfloat16)
        pieces.append(piece)
        x = x - piece.astype(jnp.float32)
    return pieces


def dot(a, b):
    return jnp.dot(a, b, preferred_element_type=jnp.float32)


def dot_lanes(a, b):
    return lax.dot_general(a, b, (((1,), (1,)), ((), ())), preferred_element_type=jnp.float32)


def dot_narrow(a, b):
    return dot(a[0], b[0]) + (dot(a[0], b[1]) + dot(a[1], b[0]))


def used_positions(lists_ref, tally_ref, start, g):
    length = lists_ref.shape[1]
    shape = (length, length)
    tallies = tally_ref[...].astype(jnp.float32)
    lane = lax.broadcasted_iota(jnp.int32, tallies.shape, 1)
    tally = jnp.sum(jnp.where(lane == g, tallies, 0.0), axis=1, keepdims=True)
    place = lists_ref[pl.ds(g, 1), :] - jnp.concatenate([start] * (length // LANES), axis=1)
    listed = lax.broadcasted_iota(jnp.int32, shape, 0) == jnp.broadcast_to(place, shape)
    listed = listed.astype(jnp.float32).astype(jnp.bfloat16)
    entry = lax.broadcasted_iota(jnp.int32, (16, length), 1).astype(jnp.float32)
    used = (entry < tally).astype(jnp.float32).astype(jnp.bfloat16)
    return dot_lanes(used, listed)[0:1]


def identity_of(members):
    rows = lax.broadcasted_iota(jnp.int32, (members, members), 0)
    lanes = lax.broadcasted_iota(jnp.int32, (members, members), 1)
    return (rows == lanes).astype(jnp.float32)


def begin_root(lines, readings, weight, g, iterate, root, factor, innovation_sum, norm):
    blocks, _, runs, _ = lines.shape
    members = blocks * runs
    observed = jnp.concatenate([lines[b, g] for b in range(blocks)], axis=0).astype(jnp.float32)
    ens_mean = jnp.sum(observed, axis=0, keepdims=True) * (1.0 / members)
    anomaly = (observed - ens_mean).astype(jnp.bfloat16)
    identity = identity_of(members)
    weighted = split(anomaly.astype(jnp.float32) * weight, 2)
    gram = dot_lanes(anomaly, weighted[0]) + dot_lanes(anomaly, weighted[1])
    gram = gram + (members - 1) / inflation * identity
    innovation = jnp.broadcast_to(weight * (readings - ens_mean), (16, weight.shape[1]))
    innovation = split(innovation, 3)
    innovation_sum[g] = sum(dot_lanes(piece, anomaly) for piece in innovation)[0:8]
    squares = jnp.sum(jnp.sum(gram * gram, axis=0, keepdims=True), axis=1, keepdims=True)
    frobenius = jnp.sqrt(squares)
    norm[g] = jnp.broadcast_to(jnp.sqrt(frobenius), norm.shape[1:])
    scaled = gram / frobenius
    first = 1.5 * identity - 0.5 * scaled
    keep(iterate, g, scaled)
    keep(factor, g, first)
    keep(root, g, first)


def keep(ref, g, value):
    ref[g, 0], ref[g, 1] = split(value, 2)


def refine_roots(iterate, root, factor):
    groups, _, members, _ = iterate.shape

    def step(i, carry):
        for g in range(groups):
            keep(iterate, g, dot_narrow(iterate[g], factor[g]))
        for g in range(groups):
            product = dot_narrow(root[g], iterate[g])
            keep(factor, g, 1.5 * identity_of(members) - 0.5 * product)
        for g in range(groups):
            keep(root, g, dot_narrow(factor[g], root[g]))
        return carry

    lax.fori_loop(1, NS_ITERS, step, 0)


def finish_transform(root, innovation_sum, norm, joined, g):
    members = root.shape[2]
    inverse_root = root[g, 0].astype(jnp.float32) + root[g, 1].astype(jnp.float32)
    inverse_root = inverse_root * (1.0 / norm[g][0:1, 0:1])
    inner = jnp.sum(inverse_root * innovation_sum[g][0:1], axis=1, keepdims=True)
    mean_weight = jnp.sum(inverse_root * inner, axis=0, keepdims=True)
    turned = math.sqrt(members - 1) * inverse_root + mean_weight
    joined[:, g * members : (g + 1) * members] = turned.astype(jnp.bfloat16)


def kernel(
    patch,
    groups,
    states_hbm,
    runs_hbm,
    readings_hbm,
    precision_hbm,
    lists_hbm,
    tally_hbm,
    result_ref,
    states_ref,
    lists_ref,
    tally_ref,
    packed,
    arrived,
    outgoing,
    received,
    extended,
    readings,
    precision,
    starts,
    all_starts,
    windows,
    lines,
    joined,
    iterate,
    root,
    factor,
    innovation_sum,
    norm,
    send_sem,
    recv_sem,
    small_send,
    small_recv,
    halo_send,
    halo_recv,
    local_sem,
):
    blocks, rows, _, _ = packed.shape
    length = lines.shape[3]
    own = runs_hbm.shape[1]
    own_columns = pl.ds(HW, own)
    me = lax.axis_index("mem")
    region = lax.axis_index("reg")
    regions = lax.axis_size("reg")
    after = {"reg": lax.rem(region + 1, regions)}
    before = {"reg": lax.rem(region + regions - 1, regions)}
    peers = [lax.rem(me + k, blocks) for k in range(1, blocks)]

    def send(source, target, sems, device):
        copy = pltpu.make_async_remote_copy(
            src_ref=source,
            dst_ref=target,
            send_sem=sems[0],
            recv_sem=sems[1],
            device_id=device,
            device_id_type=MESH,
        )
        copy.start()
        return copy

    barrier = pltpu.get_barrier_semaphore()
    for device in [{"mem": peer} for peer in peers] + [after, before]:
        pl.semaphore_signal(barrier, inc=1, device_id=device, device_id_type=MESH)
    local = []
    for i, (source, target) in enumerate(
        (
            (lists_hbm, lists_ref),
            (tally_hbm, tally_ref),
            (states_hbm, states_ref),
            (runs_hbm, extended.at[:, own_columns]),
            (readings_hbm, readings.at[:, own_columns]),
            (precision_hbm, precision.at[:, own_columns]),
        )
    ):
        copy = pltpu.make_async_copy(source, target, local_sem.at[i])
        copy.start()
        local.append(copy)
    local[0].wait()
    lowest = jnp.min(lists_ref[...].astype(jnp.float32), axis=1, keepdims=True)
    starts[...] = jnp.zeros_like(starts)
    starts[0:groups, :] = jnp.broadcast_to(lowest, (groups, LANES)).astype(jnp.int32)
    pl.semaphore_wait(barrier, blocks + 1)

    small = []
    for k, peer in enumerate(peers):
        sems = small_send.at[0, k], small_recv.at[0, k]
        small.append(send(starts, all_starts.at[me], sems, {"mem": peer}))
    last_columns, first_columns = pl.ds(own - HW, HW), pl.ds(0, HW)
    beyond = pl.ds(own + HW, HW)
    for i, (source, target) in enumerate(
        ((runs_hbm, extended), (readings_hbm, readings), (precision_hbm, precision))
    ):
        sems = halo_send.at[2 * i], halo_recv.at[2 * i]
        small.append(
            send(source.at[:, last_columns], target.at[:, first_columns], sems, after)
        )
        sems = halo_send.at[2 * i + 1], halo_recv.at[2 * i + 1]
        small.append(send(source.at[:, first_columns], target.at[:, beyond], sems, before))
    local[2].wait()

    bounds = chunk_bounds(rows)
    forward = []

    def send_states(c):
        first, last = bounds[c]
        span = pl.ds(first, last - first)
        for k, peer in enumerate(peers):
            sems = send_sem.at[0, k, c], recv_sem.at[0, k, c]
            forward.append(
                send(packed.at[peer, span], arrived.at[me, span], sems, {"mem": peer})
            )
        arrived[me, span] = packed[me, span]

    pack_rows(states_ref, packed, *bounds[0])
    send_states(0)
    for copy in local[1:2] + local[3:]:
        copy.wait()
    for copy in small:
        copy.wait_recv()

    sent_windows = []
    for k, peer in enumerate(peers):

        def cut(g, carry, peer=peer):
            windows[peer, g] = load_runs(extended, all_starts[peer, pl.ds(g, 1), :], length)
            return carry

        lax.fori_loop(0, groups, cut, 0)
        sems = small_send.at[1, k], small_recv.at[1, k]
        sent_windows.append(send(windows.at[peer], lines.at[me], sems, {"mem": peer}))

    def cut_own(g, carry):
        lines[me, g] = load_runs(extended, starts[pl.ds(g, 1), :], length)
        return carry

    lax.fori_loop(0, groups, cut_own, 0)
    pack_rows(states_ref, packed, bounds[0][1], rows)
    for copy in sent_windows:
        copy.wait_recv()
    for c in range(1, CHUNKS):
        send_states(c)

    def begin(g, carry):
        start = starts[pl.ds(g, 1), :]
        weight = load_statistics(precision, start, length)
        weight = weight * used_positions(lists_ref, tally_ref, start, g)
        observed = load_statistics(readings, start, length)
        begin_root(lines, observed, weight, g, iterate, root, factor, innovation_sum, norm)
        return carry

    lax.fori_loop(0, groups, begin, 0)
    refine_roots(iterate, root, factor)
    for g in range(groups):
        finish_transform(root, innovation_sum, norm, joined, g)

    returned = []
    for c, (first, last) in enumerate(bounds):
        for copy in forward[c * (blocks - 1) : (c + 1) * (blocks - 1)]:
            copy.wait_recv()
        apply_rows(joined, arrived, outgoing, first, last, patch, groups)
        span = pl.ds(first, last - first)
        for k, peer in enumerate(peers):
            sems = send_sem.at[1, k, c], recv_sem.at[1, k, c]
            returned.append(
                send(outgoing.at[peer, span], received.at[me, span], sems, {"mem": peer})
            )
        received[me, span] = outgoing[me, span]
    for c, (first, last) in enumerate(bounds):
        for copy in returned[c * (blocks - 1) : (c + 1) * (blocks - 1)]:
            copy.wait_recv()
        unpack_rows(received, result_ref, first, last)
    for copy in small + sent_windows + forward + returned:
        copy.wait_send()


def assimilate(states, runs, readings, precision, lists, tally, blocks):
    fields, count, columns = states.shape
    groups, length = lists.shape
    members = count * blocks
    own = runs.shape[1]
    width = columns // blocks
    rows = -(-fields // (LANES // width))
    packed = pltpu.VMEM((blocks, rows, count, LANES), jnp.bfloat16)
    square = pltpu.VMEM((groups, 2, members, members), jnp.bfloat16)
    window = pltpu.VMEM((blocks, groups, count, length), jnp.bfloat16)
    start_rows = groups + -groups % 8
    dma = pltpu.SemaphoreType.DMA
    return pl.pallas_call(
        functools.partial(kernel, width // groups, groups),
        out_shape=pltpu.VMEM(states.shape, jnp.bfloat16),
        in_specs=[pl.BlockSpec(memory_space=pltpu.HBM)] * 6,
        out_specs=pl.BlockSpec(memory_space=pltpu.VMEM),
        scratch_shapes=[
            pltpu.VMEM(states.shape, jnp.bfloat16),
            pltpu.VMEM(lists.shape, jnp.int32),
            pltpu.VMEM(tally.shape, jnp.int32),
            packed,
            packed,
            packed,
            packed,
            pltpu.VMEM((count, own + 2 * HW), jnp.bfloat16),
            pltpu.VMEM((1, own + 2 * HW), jnp.float32),
            pltpu.VMEM((1, own + 2 * HW), jnp.float32),
            pltpu.VMEM((start_rows, LANES), jnp.int32),
            pltpu.VMEM((blocks, start_rows, LANES), jnp.int32),
            window,
            window,
            pltpu.VMEM((members, groups * members), jnp.bfloat16),
            square,
            square,
            square,
            pltpu.VMEM((groups, 8, members), jnp.float32),
            pltpu.VMEM((groups, 8, LANES), jnp.float32),
            dma((2, blocks - 1, CHUNKS)),
            dma((2, blocks - 1, CHUNKS)),
            dma((2, blocks - 1)),
            dma((2, blocks - 1)),
            dma((6,)),
            dma((6,)),
            dma((6,)),
        ],
        compiler_params=pltpu.CompilerParams(
            collective_id=0, has_side_effects=True, vmem_limit_bytes=VMEM_LIMIT
        ),
        name="assimilate",
    )(
        *(
            pltpu.with_memory_space_constraint(operand, pltpu.HBM)
            for operand in (states, runs, readings, precision, lists, tally)
        )
    )


def per_device(
    prior_states,
    sensor_space_runs,
    sensor_readings,
    noise_precision,
    reading_pointers,
    reading_tally,
):
    analysed = assimilate(
        jnp.transpose(prior_states, (1, 0, 2)),
        sensor_space_runs[:, 0],
        sensor_readings,
        noise_precision,
        reading_pointers[0, 0],
        reading_tally[0],
        lax.axis_size("mem"),
    )
    return jnp.transpose(analysed, (1, 0, 2))


def solution(mesh):
    placed = (
        P("mem", None, "reg"),
        P("mem", "reg", None),
        P("reg", None),
        P("reg", None),
        P("reg", "mem", None, None),
        P("reg", "mem", None),
    )
    return jax.shard_map(
        per_device, mesh=mesh, in_specs=placed, out_specs=P("mem", None, "reg"), check_vma=False
    )
```

```python
import functools
import math

import jax
import jax.numpy as jnp
from jax import lax
from jax.experimental import pallas as pl
from jax.experimental.pallas import tpu as pltpu
from jax.sharding import PartitionSpec as P

NS_ITERS = 6
HW = 256
LANES = 128
CHUNKS = 8
EARLY = 2
VMEM_LIMIT = 48 * 1024 * 1024

inflation = 1.1
MESH = pl.DeviceIdType.MESH


def lane_part(shape, width):
    return lax.broadcasted_iota(jnp.int32, shape, len(shape) - 1) // width


def swap_lane_parts(pieces, width):
    parts = len(pieces)
    part = lane_part(pieces[0].shape, width)
    swapped = []
    for d in range(parts):
        result = pieces[d]
        for s in range(parts):
            if s != d:
                moved = pltpu.roll(pieces[s], (s - d) * width % LANES, 1)
                result = jnp.where(part == s, moved, result)
        swapped.append(result)
    return swapped


def chunk_bounds(rows):
    edges = [rows * i // CHUNKS // 2 * 2 for i in range(CHUNKS)] + [rows]
    return list(zip(edges[:-1], edges[1:]))


def apply_rows(transform_ref, states_ref, result_ref, first, last, patch, groups):
    blocks, _, runs, _ = states_ref.shape
    members = blocks * runs

    def one(r):
        x = jnp.concatenate([states_ref[b, r] for b in range(blocks)], axis=0)
        x = x.astype(jnp.float32)
        center = jnp.sum(x, axis=0, keepdims=True) * (1.0 / members)
        pert = (x - center).astype(jnp.bfloat16).astype(jnp.float32)
        group = lane_part(pert.shape, patch) % groups
        masked = [jnp.where(group == g, pert, 0.0).astype(jnp.bfloat16) for g in range(groups)]
        return center, jnp.concatenate(masked, axis=0)

    def body(i, carry):
        r0 = first + 2 * i
        r1 = jnp.minimum(r0 + 1, last - 1)
        center0, masked0 = one(r0)
        center1, masked1 = one(r1)
        moved = jnp.dot(
            transform_ref[...],
            jnp.concatenate([masked0, masked1], axis=1),
            preferred_element_type=jnp.float32,
        )
        for r, center, lanes in ((r0, center0, slice(0, LANES)), (r1, center1, slice(LANES, None))):
            analysed = (moved[:, lanes] + center).astype(jnp.bfloat16)
            for b in range(blocks):
                result_ref[b, r] = analysed[b * runs : (b + 1) * runs]
        return carry

    lax.fori_loop(0, (last - first + 1) // 2, body, 0)


def unpack_row(received, result_ref, r, valid):
    blocks, rows, _, _ = received.shape
    columns = result_ref.shape[2]
    width = columns // blocks
    parts = LANES // width
    for tile in range(columns // LANES):
        lanes = slice(tile * LANES, (tile + 1) * LANES)
        pieces = [received[tile * parts + d, r].astype(jnp.float32) for d in range(parts)]
        swapped = swap_lane_parts(pieces, width)
        for s in range(valid):
            result_ref[s * rows + r, :, lanes] = swapped[s].astype(jnp.bfloat16)


def unpack_rows(received, result_ref, first, last):
    rows = received.shape[1]
    fields = result_ref.shape[0]
    parts = LANES // (result_ref.shape[2] // received.shape[0])
    whole = rows - (parts * rows - fields)

    def body(r, carry):
        unpack_row(received, result_ref, r, parts)
        return carry

    lax.fori_loop(first, min(last, whole), body, 0)
    for r in range(max(first, whole), last):
        unpack_row(received, result_ref, r, parts - 1)


def pack_rows(states_ref, packed, first, last):
    fields, _, columns = states_ref.shape
    blocks, rows, _, _ = packed.shape
    width = columns // blocks
    parts = LANES // width

    def body(r, carry):
        for tile in range(columns // LANES):
            lanes = slice(tile * LANES, (tile + 1) * LANES)
            pieces = [
                states_ref[jnp.minimum(s * rows + r, fields - 1), :, lanes].astype(jnp.float32)
                for s in range(parts)
            ]
            for d, piece in enumerate(swap_lane_parts(pieces, width)):
                packed[tile * parts + d, r] = piece.astype(jnp.bfloat16)
        return carry

    lax.fori_loop(first, last, body, 0)


def bit_of(start, bit, shape, kind):
    value = jnp.broadcast_to((start >> bit) & 1, shape)
    return value.astype(jnp.float32).astype(kind) > 0.5


def nearest_tiles(extended, start, length):
    shape = (extended.shape[0], LANES)
    keep = length // LANES
    total = extended.shape[1] // LANES
    tiles = [extended[:, i * LANES : (i + 1) * LANES] for i in range(total)]
    for bit in reversed(range((total - keep).bit_length())):
        shift = 1 << bit
        mask = bit_of(start, bit + LANES.bit_length() - 1, shape, extended.dtype)
        tiles = [
            jnp.where(mask, tiles[i + shift], tiles[i]) if i + shift < len(tiles) else tiles[i]
            for i in range(min(len(tiles), shift + keep))
        ]
    return tiles


def load_runs(extended, start, length):
    tiles = nearest_tiles(extended, start, length)
    count = extended.shape[0]
    shape = (2 * LANES, LANES)
    row = lax.broadcasted_iota(jnp.int32, shape, 0)
    lane = lax.broadcasted_iota(jnp.int32, shape, 1)
    chosen = (row - lane == jnp.broadcast_to(start & (LANES - 1), shape)).astype(jnp.float32)
    pairs = [jnp.concatenate([a, b], axis=1) for a, b in zip(tiles[:-1], tiles[1:])]
    shifted = dot(jnp.concatenate(pairs, axis=0), chosen.astype(jnp.bfloat16))
    shifted = shifted.astype(jnp.bfloat16)
    return jnp.concatenate(
        [shifted[i * count : (i + 1) * count] for i in range(len(pairs))], axis=1
    )


def load_statistics(extended, start, length):
    tiles = nearest_tiles(extended, start, length)
    shape = tiles[0].shape
    for bit in range(LANES.bit_length() - 1):
        mask = bit_of(start, bit, shape, jnp.float32)
        tiles = [jnp.where(mask, pltpu.roll(t, LANES - (1 << bit), 1), t) for t in tiles]
    lane = lax.broadcasted_iota(jnp.int32, shape, 1)
    here = lane < LANES - jnp.broadcast_to(start & (LANES - 1), shape)
    return jnp.concatenate(
        [jnp.where(here, a, b) for a, b in zip(tiles[:-1], tiles[1:])], axis=1
    )


def split(x, terms):
    pieces = []
    for _ in range(terms):
        piece = x.astype(jnp.bfloat16)
        pieces.append(piece)
        x = x - piece.astype(jnp.float32)
    return pieces


def dot(a, b):
    return jnp.dot(a, b, preferred_element_type=jnp.float32)


def dot_lanes(a, b):
    return lax.dot_general(a, b, (((1,), (1,)), ((), ())), preferred_element_type=jnp.float32)


def dot_narrow(a, b):
    return dot(a[0], b[0]) + (dot(a[0], b[1]) + dot(a[1], b[0]))


def used_positions(lists_ref, tally_ref, start, g):
    length = lists_ref.shape[1]
    shape = (length, length)
    tallies = tally_ref[...].astype(jnp.float32)
    lane = lax.broadcasted_iota(jnp.int32, tallies.shape, 1)
    tally = jnp.sum(jnp.where(lane == g, tallies, 0.0), axis=1, keepdims=True)
    place = lists_ref[pl.ds(g, 1), :] - jnp.concatenate([start] * (length // LANES), axis=1)
    listed = lax.broadcasted_iota(jnp.int32, shape, 0) == jnp.broadcast_to(place, shape)
    listed = listed.astype(jnp.float32).astype(jnp.bfloat16)
    entry = lax.broadcasted_iota(jnp.int32, (16, length), 1).astype(jnp.float32)
    used = (entry < tally).astype(jnp.float32).astype(jnp.bfloat16)
    return dot_lanes(used, listed)[0:1]


def identity_of(members):
    rows = lax.broadcasted_iota(jnp.int32, (members, members), 0)
    lanes = lax.broadcasted_iota(jnp.int32, (members, members), 1)
    return (rows == lanes).astype(jnp.float32)


def begin_root(lines, readings, weight, g, iterate, root, factor, innovation_sum, norm):
    blocks, _, runs, _ = lines.shape
    members = blocks * runs
    observed = jnp.concatenate([lines[b, g] for b in range(blocks)], axis=0).astype(jnp.float32)
    ens_mean = jnp.sum(observed, axis=0, keepdims=True) * (1.0 / members)
    anomaly = (observed - ens_mean).astype(jnp.bfloat16)
    identity = identity_of(members)
    weighted = split(anomaly.astype(jnp.float32) * weight, 2)
    gram = dot_lanes(anomaly, weighted[0]) + dot_lanes(anomaly, weighted[1])
    gram = gram + (members - 1) / inflation * identity
    innovation = jnp.broadcast_to(weight * (readings - ens_mean), (16, weight.shape[1]))
    innovation = split(innovation, 3)
    innovation_sum[g] = sum(dot_lanes(piece, anomaly) for piece in innovation)[0:8]
    squares = jnp.sum(jnp.sum(gram * gram, axis=0, keepdims=True), axis=1, keepdims=True)
    frobenius = jnp.sqrt(squares)
    norm[g] = jnp.broadcast_to(jnp.sqrt(frobenius), norm.shape[1:])
    scaled = gram / frobenius
    first = 1.5 * identity - 0.5 * scaled
    keep(iterate, g, scaled)
    keep(factor, g, first)
    keep(root, g, first)


def keep(ref, g, value):
    ref[g, 0], ref[g, 1] = split(value, 2)


def refine_roots(iterate, root, factor):
    groups, _, members, _ = iterate.shape

    def step(i, carry):
        for g in range(groups):
            keep(iterate, g, dot_narrow(iterate[g], factor[g]))
        for g in range(groups):
            product = dot_narrow(root[g], iterate[g])
            keep(factor, g, 1.5 * identity_of(members) - 0.5 * product)
        for g in range(groups):
            keep(root, g, dot_narrow(factor[g], root[g]))
        return carry

    lax.fori_loop(1, NS_ITERS, step, 0)


def finish_transform(root, innovation_sum, norm, joined, g):
    members = root.shape[2]
    inverse_root = root[g, 0].astype(jnp.float32) + root[g, 1].astype(jnp.float32)
    inverse_root = inverse_root * (1.0 / norm[g][0:1, 0:1])
    inner = jnp.sum(inverse_root * innovation_sum[g][0:1], axis=1, keepdims=True)
    mean_weight = jnp.sum(inverse_root * inner, axis=0, keepdims=True)
    turned = math.sqrt(members - 1) * inverse_root + mean_weight
    joined[:, g * members : (g + 1) * members] = turned.astype(jnp.bfloat16)


def kernel(
    patch,
    groups,
    states_hbm,
    runs_hbm,
    readings_hbm,
    precision_hbm,
    lists_hbm,
    tally_hbm,
    result_ref,
    states_ref,
    lists_ref,
    tally_ref,
    packed,
    arrived,
    outgoing,
    received,
    extended,
    readings,
    precision,
    starts,
    all_starts,
    windows,
    lines,
    joined,
    iterate,
    root,
    factor,
    innovation_sum,
    norm,
    send_sem,
    recv_sem,
    small_send,
    small_recv,
    halo_send,
    halo_recv,
    local_sem,
):
    blocks, rows, _, _ = packed.shape
    length = lines.shape[3]
    own = runs_hbm.shape[1]
    own_columns = pl.ds(HW, own)
    me = lax.axis_index("mem")
    region = lax.axis_index("reg")
    regions = lax.axis_size("reg")
    after = {"reg": lax.rem(region + 1, regions)}
    before = {"reg": lax.rem(region + regions - 1, regions)}
    peers = [lax.rem(me + k, blocks) for k in range(1, blocks)]

    def send(source, target, sems, device):
        copy = pltpu.make_async_remote_copy(
            src_ref=source,
            dst_ref=target,
            send_sem=sems[0],
            recv_sem=sems[1],
            device_id=device,
            device_id_type=MESH,
        )
        copy.start()
        return copy

    barrier = pltpu.get_barrier_semaphore()
    for device in [{"mem": peer} for peer in peers] + [after, before]:
        pl.semaphore_signal(barrier, inc=1, device_id=device, device_id_type=MESH)
    local = []
    for i, (source, target) in enumerate(
        (
            (lists_hbm, lists_ref),
            (tally_hbm, tally_ref),
            (states_hbm, states_ref),
            (runs_hbm, extended.at[:, own_columns]),
            (readings_hbm, readings.at[:, own_columns]),
            (precision_hbm, precision.at[:, own_columns]),
        )
    ):
        copy = pltpu.make_async_copy(source, target, local_sem.at[i])
        copy.start()
        local.append(copy)
    local[0].wait()
    lowest = jnp.min(lists_ref[...].astype(jnp.float32), axis=1, keepdims=True)
    starts[...] = jnp.zeros_like(starts)
    starts[0:groups, :] = jnp.broadcast_to(lowest, (groups, LANES)).astype(jnp.int32)
    pl.semaphore_wait(barrier, blocks + 1)

    small = []
    for k, peer in enumerate(peers):
        sems = small_send.at[0, k], small_recv.at[0, k]
        small.append(send(starts, all_starts.at[me], sems, {"mem": peer}))
    last_columns, first_columns = pl.ds(own - HW, HW), pl.ds(0, HW)
    beyond = pl.ds(own + HW, HW)
    for i, (source, target) in enumerate(
        ((runs_hbm, extended), (readings_hbm, readings), (precision_hbm, precision))
    ):
        sems = halo_send.at[2 * i], halo_recv.at[2 * i]
        small.append(
            send(source.at[:, last_columns], target.at[:, first_columns], sems, after)
        )
        sems = halo_send.at[2 * i + 1], halo_recv.at[2 * i + 1]
        small.append(send(source.at[:, first_columns], target.at[:, beyond], sems, before))
    local[2].wait()

    bounds = chunk_bounds(rows)
    forward = []

    def exchange_states(c):
        first, last = bounds[c]
        pack_rows(states_ref, packed, first, last)
        span = pl.ds(first, last - first)
        for k, peer in enumerate(peers):
            sems = send_sem.at[0, k, c], recv_sem.at[0, k, c]
            forward.append(
                send(packed.at[peer, span], arrived.at[me, span], sems, {"mem": peer})
            )
        arrived[me, span] = packed[me, span]

    for c in range(EARLY):
        exchange_states(c)
    for copy in local[1:2] + local[3:]:
        copy.wait()
    for copy in small:
        copy.wait_recv()

    sent_windows = []
    for k, peer in enumerate(peers):

        def cut(g, carry, peer=peer):
            windows[peer, g] = load_runs(extended, all_starts[peer, pl.ds(g, 1), :], length)
            return carry

        lax.fori_loop(0, groups, cut, 0)
        sems = small_send.at[1, k], small_recv.at[1, k]
        sent_windows.append(send(windows.at[peer], lines.at[me], sems, {"mem": peer}))

    def cut_own(g, carry):
        lines[me, g] = load_runs(extended, starts[pl.ds(g, 1), :], length)
        return carry

    lax.fori_loop(0, groups, cut_own, 0)
    for c in range(EARLY, CHUNKS):
        exchange_states(c)
    for copy in sent_windows:
        copy.wait_recv()

    def begin(g, carry):
        start = starts[pl.ds(g, 1), :]
        weight = load_statistics(precision, start, length)
        weight = weight * used_positions(lists_ref, tally_ref, start, g)
        observed = load_statistics(readings, start, length)
        begin_root(lines, observed, weight, g, iterate, root, factor, innovation_sum, norm)
        return carry

    lax.fori_loop(0, groups, begin, 0)
    refine_roots(iterate, root, factor)
    for g in range(groups):
        finish_transform(root, innovation_sum, norm, joined, g)

    returned = []
    for c, (first, last) in enumerate(bounds):
        for copy in forward[c * (blocks - 1) : (c + 1) * (blocks - 1)]:
            copy.wait_recv()
        apply_rows(joined, arrived, outgoing, first, last, patch, groups)
        span = pl.ds(first, last - first)
        for k, peer in enumerate(peers):
            sems = send_sem.at[1, k, c], recv_sem.at[1, k, c]
            returned.append(
                send(outgoing.at[peer, span], received.at[me, span], sems, {"mem": peer})
            )
        received[me, span] = outgoing[me, span]
    for c, (first, last) in enumerate(bounds):
        for copy in returned[c * (blocks - 1) : (c + 1) * (blocks - 1)]:
            copy.wait_recv()
        unpack_rows(received, result_ref, first, last)
    for copy in small + sent_windows + forward + returned:
        copy.wait_send()


def assimilate(states, runs, readings, precision, lists, tally, blocks):
    fields, count, columns = states.shape
    groups, length = lists.shape
    members = count * blocks
    own = runs.shape[1]
    width = columns // blocks
    rows = -(-fields // (LANES // width))
    packed = pltpu.VMEM((blocks, rows, count, LANES), jnp.bfloat16)
    square = pltpu.VMEM((groups, 2, members, members), jnp.bfloat16)
    window = pltpu.VMEM((blocks, groups, count, length), jnp.bfloat16)
    start_rows = groups + -groups % 8
    dma = pltpu.SemaphoreType.DMA
    return pl.pallas_call(
        functools.partial(kernel, width // groups, groups),
        out_shape=pltpu.VMEM(states.shape, jnp.bfloat16),
        in_specs=[pl.BlockSpec(memory_space=pltpu.HBM)] * 6,
        out_specs=pl.BlockSpec(memory_space=pltpu.VMEM),
        scratch_shapes=[
            pltpu.VMEM(states.shape, jnp.bfloat16),
            pltpu.VMEM(lists.shape, jnp.int32),
            pltpu.VMEM(tally.shape, jnp.int32),
            packed,
            packed,
            packed,
            packed,
            pltpu.VMEM((count, own + 2 * HW), jnp.bfloat16),
            pltpu.VMEM((1, own + 2 * HW), jnp.float32),
            pltpu.VMEM((1, own + 2 * HW), jnp.float32),
            pltpu.VMEM((start_rows, LANES), jnp.int32),
            pltpu.VMEM((blocks, start_rows, LANES), jnp.int32),
            window,
            window,
            pltpu.VMEM((members, groups * members), jnp.bfloat16),
            square,
            square,
            square,
            pltpu.VMEM((groups, 8, members), jnp.float32),
            pltpu.VMEM((groups, 8, LANES), jnp.float32),
            dma((2, blocks - 1, CHUNKS)),
            dma((2, blocks - 1, CHUNKS)),
            dma((2, blocks - 1)),
            dma((2, blocks - 1)),
            dma((6,)),
            dma((6,)),
            dma((6,)),
        ],
        compiler_params=pltpu.CompilerParams(
            collective_id=0, has_side_effects=True, vmem_limit_bytes=VMEM_LIMIT
        ),
        name="assimilate",
    )(
        *(
            pltpu.with_memory_space_constraint(operand, pltpu.HBM)
            for operand in (states, runs, readings, precision, lists, tally)
        )
    )


def per_device(
    prior_states,
    sensor_space_runs,
    sensor_readings,
    noise_precision,
    reading_pointers,
    reading_tally,
):
    analysed = assimilate(
        jnp.transpose(prior_states, (1, 0, 2)),
        sensor_space_runs[:, 0],
        sensor_readings,
        noise_precision,
        reading_pointers[0, 0],
        reading_tally[0],
        lax.axis_size("mem"),
    )
    return jnp.transpose(analysed, (1, 0, 2))


def solution(mesh):
    placed = (
        P("mem", None, "reg"),
        P("mem", "reg", None),
        P("reg", None),
        P("reg", None),
        P("reg", "mem", None, None),
        P("reg", "mem", None),
    )
    return jax.shard_map(
        per_device, mesh=mesh, in_specs=placed, out_specs=P("mem", None, "reg"), check_vma=False
    )
```
